32 devices in a mesh: groups: 2 (over x), shard: 16 (over z, y, core).
Axes of the slice: x: 2, y: 2, z: 4, core: 2. Of those that a mesh axis runs over, the one named last changes fastest.
Arguments:
- queries: bfloat16 [256, 32, 128], P(('groups', 'shard')), parts along dimension 0, may hold values from -2 to 2
- passages: bfloat16 [8192, 180, 128], P(('groups', 'shard')), parts along dimension 0, may hold values from -2 to 2
- lengths: int32 [8192], P(('groups', 'shard')), parts along dimension 0, may hold values from 45 to 180
- candidates: int32 [256, 256], P(('groups', 'shard')), parts along dimension 0, may hold values from 0 to 4095, as said below
- placement: int32 [8192], P('groups'), parts along dimension 0, may hold values from 0 to 4095, as said below
Outputs:
- scores: float32 [256, 256], P(('groups', 'shard')), parts along dimension 0
The draws below stay inside these ranges and needn't reach their ends.
There are 2 independent parts, one for each index of `groups`. The reference program is written for one: setup_inputs(seed, part) draws one part's arguments, and reference() takes and returns one part's arrays. A program takes and returns all parts, laid end to end along the dimension named above; each array names one. Nothing has to cross between parts.
Inputs may be any that keep to these rules, and one draw needn't show every extreme that they name: placement is a permutation; a passage in slot s is stored on device s // 256 of the shard axis, row s % 256 of that device's passages. Within a part, no passage is named by more than 16 entries of candidates, and some passage by exactly 16; every passage is named at least once; a query may name a passage twice. The entries of the 8 queries of one device that name passages stored on one device number at most 256, and exactly 256 for some storing device.
All inputs are finite; a program needn't handle non-finite values.
Results may differ from the reference program's by a relative error of at most 0.0003.
Values may be sent and summed in bfloat16 or wider, within the bound.
No kernel may reach another device: no remote copies, remote signals or barrier semaphores. Data moves between devices by JAX's collectives and lax.ppermute only.
A program may use at most 128 MiB of HBM per device.

```python
import jax
import jax.numpy as jnp
from jax import lax

DIM = 128
QT = 32
PT = 180
Q_DEV = 8
PASS_DEV = 256
CAND = 256
PMOST = 16
QUERIES = 128
PASSAGES = 4096
N_SHARD = 16


def routing_tables(key):
    keys = jax.random.split(key, 6)
    slots = jnp.arange(PASSAGES, dtype=jnp.int32)
    stored = jax.random.permutation(keys[0], PASSAGES).astype(jnp.int32)
    hot_device = jax.random.randint(keys[1], (), 0, N_SHARD)
    on_hot = slots // PASS_DEV == hot_device
    hot_total = PASS_DEV * PMOST
    remaining = QUERIES * CAND - hot_total
    weights = jnp.where(on_hot, 0, jax.random.randint(keys[4], (PASSAGES,), 3, 6))
    weight_sum = jnp.sum(weights)
    base_counts = remaining * weights // weight_sum
    leftover = remaining - jnp.sum(base_counts)
    other_rank = jnp.cumsum(jnp.where(on_hot, 0, 1)) - 1
    extra = jnp.where(jnp.logical_and(jnp.logical_not(on_hot), other_rank < leftover), 1, 0)
    counts = jnp.where(on_hot, PMOST, base_counts + extra).astype(jnp.int32)
    listing = jnp.repeat(slots, counts, total_repeat_length=QUERIES * CAND)
    dealt = listing.reshape(Q_DEV * CAND, N_SHARD).T
    row_keys = jax.random.split(keys[5], N_SHARD)
    dealt = jax.vmap(lambda row_key, row: jax.random.permutation(row_key, row))(row_keys, dealt)
    candidates = stored[dealt.reshape(QUERIES * CAND)].reshape(QUERIES, CAND).astype(jnp.int32)
    placement = jnp.zeros((PASSAGES,), jnp.int32).at[stored].set(slots)
    return (placement, candidates)


def draw_candidates(key, part):
    placement, candidates = routing_tables(key)
    return candidates


def draw_placement(key, part):
    placement, candidates = routing_tables(key)
    return placement


def draw_lengths(key, part):
    key = jax.random.fold_in(key, 11)
    first_key, second_key = jax.random.split(key)
    values = jax.random.randint(first_key, (PASSAGES,), PT // 4, PT + 1).astype(jnp.int32)
    chosen = jax.random.randint(second_key, (), 0, PASSAGES)
    values = values.at[chosen].set(PT)
    values = values.at[(chosen + 1) % PASSAGES].set(PT // 4)
    return values


def block_levels(own_key, dims, cuts, low, top_value):
    loudness, own = 1.0, jax.random.fold_in(own_key, 6)
    for position, parts in cuts:
        draws = jnp.exp(jax.random.uniform(jax.random.fold_in(own, position), (parts,), jnp.float32, low / len(cuts), top_value / len(cuts)))
        loudness = loudness * jnp.repeat(draws, dims[position] // parts).reshape([-1 if axis == position else 1 for axis in range(len(dims))])
    return loudness


def bell_draw(key, dims, width, bound, cuts=(), held_as=jnp.bfloat16):
    level = block_levels(key, dims, cuts, -0.22, 0.18) if cuts else 1.0
    result = jax.random.normal(key, dims, jnp.float32) * width * level
    return jnp.minimum(jnp.maximum(result, -bound), bound).astype(held_as)


def setup_inputs(seed: int = 0, part: int = 0) -> dict:
    streams_of = jax.random.split(jax.random.key(seed), 6)
    part_splits = jax.random.split(jax.random.fold_in(streams_of[5], part), 6)
    return {
        "queries": bell_draw(part_splits[0], (QUERIES, QT, DIM), 0.3, 2.0, ((0, 16),)),
        "passages": bell_draw(part_splits[1], (PASSAGES, PT, DIM), 0.3, 2.0, ((0, 16),)),
        "lengths": draw_lengths(jax.random.fold_in(jax.random.fold_in(streams_of[5], part), 71), part),
        "candidates": draw_candidates(jax.random.fold_in(jax.random.fold_in(streams_of[5], part), 71), part),
        "placement": draw_placement(jax.random.fold_in(jax.random.fold_in(streams_of[5], part), 71), part),
    }


def reference(queries, passages, lengths, candidates, placement):
    slot_index = placement[candidates]
    positions = jnp.arange(PT, dtype=jnp.int32)

    def score_query(inputs):
        query_block, query_slots = inputs
        documents = passages[query_slots].astype(jnp.float32)
        similar = jnp.einsum("qd,cpd->cqp", query_block.astype(jnp.float32), documents)
        live_tokens = positions[None, :] < lengths[query_slots][:, None]
        similar = jnp.where(live_tokens[:, None, :], similar, -1e30)
        closest = jnp.max(similar, axis=2)
        return jnp.mean(closest, axis=1)

    return lax.map(score_query, (queries, slot_index))
```

```python
import functools

import jax
import jax.numpy as jnp
from jax import lax
from jax.experimental import pallas as pl
from jax.experimental.pallas import tpu as pltpu
from jax.sharding import PartitionSpec as P

PMOST = 16
LANES = 128
F32 = jnp.float32
BF16 = jnp.bfloat16
I32 = jnp.int32
NT = (((1,), (1,)), ((), ()))
NN = (((1,), (0,)), ((), ()))
VMEM = pltpu.VMEM
SMEM = pltpu.SMEM
MIB = 2**20


def iota(shape, axis):
    return lax.broadcasted_iota(I32, shape, axis)


def dot(a, b, dims, **kw):
    return lax.dot_general(a, b, dims, preferred_element_type=F32, **kw)


def lookup(table, index):
    parts = []
    for c in range(index.shape[1] // LANES):
        ids = index[:, c * LANES : (c + 1) * LANES]
        lo, hi = ids & (LANES - 1), ids >> 7
        found = jnp.zeros(ids.shape, table[0].dtype)
        for t, tile in enumerate(table):
            got = jnp.take_along_axis(tile, lo, axis=1, mode="promise_in_bounds")
            found = jnp.where(hi == t, got, found)
        parts.append(found)
    return jnp.concatenate(parts, axis=1)


def route_kernel(queries_ref, cand_ref, place_ref, slot_ref, load_ref):
    q_dev, cand = cand_ref.shape
    rows = place_ref.shape[0]
    tokens = queries_ref.shape[0]
    table = [jnp.broadcast_to(place_ref[t : t + 1, :], (q_dev, LANES)) for t in range(rows)]
    slot = lookup(table, cand_ref[...])
    slot_ref[...] = slot
    bits = jnp.zeros((rows, LANES), F32)
    for q in range(q_dev):
        line = slot[q : q + 1, :]
        hi = jnp.where(iota((rows, cand), 0) == (line >> 7), 1.0, 0.0).astype(BF16)
        lo = jnp.where(iota((LANES, cand), 0) == (line & (LANES - 1)), 1.0, 0.0).astype(BF16)
        bits = bits + jnp.where(dot(hi, lo, NT) > 0.5, float(2**q), 0.0)
    load_ref[:tokens, :] = queries_ref[...]
    load_ref[tokens:, :] = bits.astype(BF16)


def turn_kernel(len_ref, in_ref, out_ref):
    tokens, group, d = in_ref.shape
    start = pl.program_id(0) * group
    r, c = iota((group * 16, group * 16), 0), iota((group * 16, group * 16), 1)
    perm = jnp.where(c == (r % 16) * group + r // 16, 1.0, 0.0).astype(BF16)
    first = [None] * group
    for t0 in range(0, tokens, 16):
        n = min(16, tokens - t0)
        x = in_ref[t0 : t0 + n].reshape(n * group, d)
        y = dot(perm[:, : n * group], x, NN)
        for p in range(group):
            rows = y[p * 16 : (p + 1) * 16]
            if t0 == 0:
                first[p] = rows[0:1]
            rows = jnp.where(iota((16, d), 0) < len_ref[start + p] - t0, rows, first[p])
            out_ref[p, t0 : t0 + 16] = rows.astype(BF16)


def score_kernel(n, unroll, me_ref, *refs):
    loads, (pas_ref, out_ref, q_ref, list_vmem, list_smem, best_ref, sem) = refs[:n], refs[n:]
    held = pas_ref.shape[0]
    rows = n * held // LANES
    tokens = loads[0].shape[0] - rows
    per = held // LANES
    q_dev = out_ref.shape[1]
    qt = tokens // q_dev
    total = n * q_dev
    me = me_ref[0]
    for k in range(n):
        q_ref[k * tokens : (k + 1) * tokens, :] = loads[k][:tokens, :]
    bits = jnp.concatenate([loads[k][tokens:, :] for k in range(n)], axis=0)
    halves = []
    for h in range(per):
        pick = iota((n, n * rows), 1) == iota((n, n * rows), 0) * rows + me * per + h
        halves.append(dot(jnp.where(pick, 1.0, 0.0).astype(BF16), bits, NN))
    masks = jnp.concatenate(halves, axis=1).astype(I32)
    named = [
        (jnp.broadcast_to(masks[k : k + 1], (q_dev, held)) >> iota((q_dev, held), 0)) & 1
        for k in range(n)
    ]
    named = jnp.concatenate(named, axis=0)
    below = jnp.where(iota((total, total), 0) > iota((total, total), 1), 1.0, 0.0).astype(BF16)
    rank = dot(below, named.astype(F32).astype(BF16), NN)
    rank = jnp.where(named > 0, rank, -1.0)
    ids = iota((total, held), 0).astype(F32)
    lines = [
        jnp.sum(jnp.where(rank == float(r), ids, 0.0), axis=0, keepdims=True) for r in range(PMOST)
    ]
    list_vmem[...] = jnp.concatenate(lines, axis=0).astype(I32) * qt
    copy = pltpu.make_async_copy(list_vmem, list_smem, sem)
    copy.start()
    copy.wait()

    def step(i, carry):
        for g in range(0, unroll, 8):
            best = []
            for u in range(g, g + 8):
                p = i * unroll + u
                block = jnp.concatenate(
                    [q_ref[pl.ds(pl.multiple_of(list_smem[r, p], qt), qt), :] for r in range(PMOST)],
                    axis=0,
                )
                best.append(jnp.max(dot(pas_ref[p], block, NT), axis=0, keepdims=True))
            at = pl.multiple_of(i * unroll + g, 8)
            best_ref[pl.ds(at, 8), :] = jnp.concatenate(best, axis=0)
        return carry

    lax.fori_loop(0, held // unroll, step, 0)
    wide = PMOST * qt
    mean = jnp.where(iota((PMOST, wide), 1) // qt == iota((PMOST, wide), 0), 1.0 / qt, 0.0)
    score = dot(mean, best_ref[...], NT, precision=lax.Precision.HIGHEST)
    dense = jnp.zeros((total, held), F32)
    for r in range(PMOST):
        dense = jnp.where(rank == float(r), score[r : r + 1, :], dense)
    for k in range(n):
        out_ref[me ^ k] = dense[k * q_dev : (k + 1) * q_dev]


def pick_kernel(slot_ref, back_ref, out_ref):
    n, _, held = back_ref.shape
    table = [
        back_ref[s][:, h * LANES : (h + 1) * LANES] for s in range(n) for h in range(held // LANES)
    ]
    out_ref[...] = lookup(table, slot_ref[...])


def spec(space):
    return pl.BlockSpec(memory_space=space)


def spread(x, n):
    def swap(v, k):
        return lax.ppermute(v, "shard", [(i, i ^ k) for i in range(n)])

    blocks = {0: x}
    for k in range(4, n, 4):
        blocks[k] = swap(x, k)
    for k in range(0, n, 4):
        blocks[k + 2] = swap(blocks[k], 2)
    for k in range(0, n, 2):
        blocks[k + 1] = swap(blocks[k], 1)
    return [blocks[k] for k in range(n)]


def shards(queries, passages, lengths, candidates, placement):
    n = lax.axis_size("shard")
    q_dev, qt, d = queries.shape
    held, pt, _ = passages.shape
    cand = candidates.shape[1]
    me = lax.axis_index("shard").astype(I32).reshape(1)
    rows = n * held // LANES
    tokens = q_dev * qt
    padded = (pt + 15) // 16 * 16
    slot, load = pl.pallas_call(
        route_kernel,
        out_shape=(
            jax.ShapeDtypeStruct((q_dev, cand), I32),
            jax.ShapeDtypeStruct((tokens + rows, d), BF16),
        ),
        name="route",
    )(queries.reshape(tokens, d), candidates, placement.reshape(rows, LANES))
    turned = pl.pallas_call(
        turn_kernel,
        grid=(held // 16,),
        in_specs=[spec(SMEM), pl.BlockSpec((pt, 16, d), lambda i: (0, i, 0))],
        out_specs=pl.BlockSpec((16, padded, d), lambda i: (i, 0, 0)),
        out_shape=jax.ShapeDtypeStruct((held, padded, d), BF16),
        cost_estimate=pl.CostEstimate(
            flops=2 * held * padded * d * 256, bytes_accessed=held * padded * d * 4, transcendentals=0
        ),
        name="turn",
    )(lengths, passages.transpose(1, 0, 2))
    loads = spread(load, n)
    dense = pl.pallas_call(
        functools.partial(score_kernel, n, 16),
        out_shape=jax.ShapeDtypeStruct((n, q_dev, held), F32),
        in_specs=[spec(SMEM)] + [spec(VMEM)] * (n + 1),
        scratch_shapes=[
            VMEM((n * tokens, d), BF16),
            VMEM((PMOST, held), I32),
            SMEM((PMOST, held), I32),
            VMEM((held, PMOST * qt), F32),
            pltpu.SemaphoreType.DMA,
        ],
        compiler_params=pltpu.CompilerParams(vmem_limit_bytes=48 * MIB),
        name="score",
    )(me, *loads, turned)
    back = lax.all_to_all(dense, "shard", split_axis=0, concat_axis=0, tiled=True)
    return pl.pallas_call(
        pick_kernel, out_shape=jax.ShapeDtypeStruct((q_dev, cand), F32), name="pick"
    )(slot, back)


def solution(mesh):
    in_specs = (
        P(("groups", "shard"), None, None),
        P(("groups", "shard"), None, None),
        P(("groups", "shard")),
        P(("groups", "shard"), None),
        P("groups"),
    )
    out_specs = P(("groups", "shard"), None)
    return jax.shard_map(shards, mesh=mesh, in_specs=in_specs, out_specs=out_specs, check_vma=False)
```

```python
import functools

import jax
import jax.numpy as jnp
from jax import lax
from jax.experimental import pallas as pl
from jax.experimental.pallas import tpu as pltpu
from jax.sharding import PartitionSpec as P

PMOST = 16
LEAST = 45
PITCH = 24
LANES = 128
F32 = jnp.float32
BF16 = jnp.bfloat16
I32 = jnp.int32
NT = (((1,), (1,)), ((), ()))
NN = (((1,), (0,)), ((), ()))
VMEM = pltpu.VMEM
SMEM = pltpu.SMEM
MIB = 2**20


def iota(shape, axis):
    return lax.broadcasted_iota(I32, shape, axis)


def dot(a, b, dims, **kw):
    return lax.dot_general(a, b, dims, preferred_element_type=F32, **kw)


def lookup(table, index):
    parts = []
    for c in range(index.shape[1] // LANES):
        ids = index[:, c * LANES : (c + 1) * LANES]
        lo, hi = ids & (LANES - 1), ids >> 7
        found = jnp.zeros(ids.shape, table[0].dtype)
        for t, tile in enumerate(table):
            got = jnp.take_along_axis(tile, lo, axis=1, mode="promise_in_bounds")
            found = jnp.where(hi == t, got, found)
        parts.append(found)
    return jnp.concatenate(parts, axis=1)


def route_kernel(queries_ref, cand_ref, place_ref, slot_ref, load_ref):
    q_dev, cand = cand_ref.shape
    rows = place_ref.shape[0]
    tokens = queries_ref.shape[0]
    table = [jnp.broadcast_to(place_ref[t : t + 1, :], (q_dev, LANES)) for t in range(rows)]
    slot = lookup(table, cand_ref[...])
    slot_ref[...] = slot
    bits = jnp.zeros((rows, LANES), F32)
    for q in range(q_dev):
        line = slot[q : q + 1, :]
        hi = jnp.where(iota((rows, cand), 0) == (line >> 7), 1.0, 0.0).astype(BF16)
        lo = jnp.where(iota((LANES, cand), 0) == (line & (LANES - 1)), 1.0, 0.0).astype(BF16)
        bits = bits + jnp.where(dot(hi, lo, NT) > 0.5, float(2**q), 0.0)
    load_ref[:tokens, :] = queries_ref[...]
    load_ref[tokens:, :] = bits.astype(BF16)


def turn(len_ref, in_ref, out_ref, wide_ref):
    tokens, held, d = in_ref.shape

    def group(g, carry):
        p0 = pl.multiple_of(g * 16, 16)
        for t in range(tokens):
            wide_ref[t * PITCH : t * PITCH + 16, :] = in_ref[t, pl.ds(p0, 16), :].astype(F32)
        for p in range(16):
            first = wide_ref[p : p + 1, :]
            length = len_ref[p0 + p]
            for t in range(0, tokens, 16):
                rows = wide_ref[pl.ds(p + t * PITCH, 16, stride=PITCH), :]
                if t + 16 > LEAST:
                    rows = jnp.where(iota((16, d), 0) < length - t, rows, first)
                out_ref[p0 + p, t : t + 16] = rows.astype(BF16)
        return carry

    lax.fori_loop(0, held // 16, group, 0)


def score_kernel(n, me_ref, count_ref, len_ref, *refs):
    loads, refs = refs[:n], refs[n:]
    in_ref, out_ref, pas_ref, wide_ref, q_ref, list_vmem, list_smem, best_ref, sem = refs
    held, padded, _ = pas_ref.shape
    rows = n * held // LANES
    tokens = loads[0].shape[0] - rows
    per = held // LANES
    q_dev = out_ref.shape[1]
    qt = tokens // q_dev
    total = n * q_dev
    low, high = (LEAST + 15) // 16, padded // 16
    me = me_ref[0]
    size = jnp.clip((len_ref[...] + 15) // 16, low, high)
    level = iota((16, held), 0)
    member = size == level
    before = jnp.where(iota((held, held), 0) < iota((held, held), 1), 1.0, 0.0).astype(BF16)
    within = dot(jnp.where(member, 1.0, 0.0).astype(BF16), before, NN)
    less = jnp.sum(jnp.where(size < level, 1.0, 0.0), axis=1, keepdims=True)
    upto = jnp.sum(jnp.where(size <= level, 1.0, 0.0), axis=1, keepdims=True)
    place = jnp.sum(jnp.where(member, less + within, 0.0), axis=0, keepdims=True)
    order = jnp.where(iota((held, held), 0) == place.astype(I32), 1.0, 0.0)
    order16 = order.astype(BF16)

    bits = jnp.concatenate([loads[k][tokens:, :] for k in range(n)], axis=0)
    halves = []
    for h in range(per):
        pick = iota((n, n * rows), 1) == iota((n, n * rows), 0) * rows + me * per + h
        halves.append(dot(jnp.where(pick, 1.0, 0.0).astype(BF16), bits, NN))
    masks = jnp.concatenate(halves, axis=1).astype(I32)
    named = [
        (jnp.broadcast_to(masks[k : k + 1], (q_dev, held)) >> iota((q_dev, held), 0)) & 1
        for k in range(n)
    ]
    named = jnp.concatenate(named, axis=0).astype(F32)
    below = jnp.where(iota((total, total), 0) > iota((total, total), 1), 1.0, 0.0).astype(BF16)
    rank = jnp.where(named > 0.5, dot(below, named.astype(BF16), NN) + 1.0, 0.0)
    ranked = dot(rank.astype(BF16), order16, NT)
    ids = iota((total, held), 0).astype(F32)
    lines = [
        jnp.sum(jnp.where(ranked == r + 1.0, ids, 0.0), axis=0, keepdims=True) for r in range(PMOST)
    ]
    list_vmem[0:PMOST, :] = jnp.concatenate(lines, axis=0).astype(I32) * qt
    own = dot(iota((16, held), 1).astype(F32).astype(BF16), order16, NT)
    list_vmem[PMOST : PMOST + 16, :] = own.astype(I32)
    list_vmem[PMOST + 16 :, :] = jnp.broadcast_to(upto, (16, held)).astype(I32)
    copy = pltpu.make_async_copy(list_vmem, list_smem, sem)
    copy.start()
    for k in range(n):
        q_ref[k * tokens : (k + 1) * tokens, :] = loads[k][:tokens, :]
    turn(count_ref, in_ref, pas_ref, wide_ref)
    copy.wait()

    def walk(size, i, carry):
        for g in (0, 8):
            best = []
            for u in range(g, g + 8):
                at = i * 16 + u
                block = jnp.concatenate(
                    [q_ref[pl.ds(pl.multiple_of(list_smem[r, at], qt), qt), :] for r in range(PMOST)],
                    axis=0,
                )
                part = pas_ref[list_smem[PMOST, at], : size * 16]
                best.append(jnp.max(dot(part, block, NT), axis=0, keepdims=True))
            at = pl.multiple_of(i * 16 + g, 8)
            best_ref[pl.ds(at, 8), :] = jnp.concatenate(best, axis=0)
        return carry

    start = 0
    for s in range(low, high + 1):
        stop = list_smem[PMOST + 16 + s, 0] // 16
        lax.fori_loop(start, stop, functools.partial(walk, s), 0)
        start = stop
    wide = PMOST * qt
    mean = jnp.where(iota((PMOST, wide), 1) // qt == iota((PMOST, wide), 0), 1.0 / qt, 0.0)
    score = dot(mean, best_ref[...], NT, precision=lax.Precision.HIGHEST)
    score = dot(score, order, NN, precision=lax.Precision.HIGHEST)
    dense = jnp.zeros((total, held), F32)
    for r in range(PMOST):
        dense = jnp.where(rank == r + 1.0, score[r : r + 1, :], dense)
    for k in range(n):
        out_ref[me ^ k] = dense[k * q_dev : (k + 1) * q_dev]


def pick_kernel(slot_ref, back_ref, out_ref):
    n, _, held = back_ref.shape
    table = [
        back_ref[s][:, h * LANES : (h + 1) * LANES] for s in range(n) for h in range(held // LANES)
    ]
    out_ref[...] = lookup(table, slot_ref[...])


def spec(space):
    return pl.BlockSpec(memory_space=space)


def swap(v, k, n):
    return lax.ppermute(v, "shard", [(i, i ^ k) for i in range(n)])


def shards(queries, passages, lengths, candidates, placement):
    n = lax.axis_size("shard")
    q_dev, qt, d = queries.shape
    held, pt, _ = passages.shape
    cand = candidates.shape[1]
    me = lax.axis_index("shard").astype(I32).reshape(1)
    rows = n * held // LANES
    tokens = q_dev * qt
    padded = (pt + 15) // 16 * 16
    slot, load = pl.pallas_call(
        route_kernel,
        out_shape=(
            jax.ShapeDtypeStruct((q_dev, cand), I32),
            jax.ShapeDtypeStruct((tokens + rows, d), BF16),
        ),
        name="route",
    )(queries.reshape(tokens, d), candidates, placement.reshape(rows, LANES))
    blocks = {0: load}
    for k in range(4, n, 4):
        blocks[k] = swap(load, k, n)
    blocks[2] = swap(load, 2, n)
    blocks[1] = swap(load, 1, n)
    for k in range(4, n, 4):
        blocks[k + 2] = swap(blocks[k], 2, n)
    for k in range(2, n, 2):
        blocks[k + 1] = swap(blocks[k], 1, n)
    loads = [blocks[k] for k in range(n)]
    dense = pl.pallas_call(
        functools.partial(score_kernel, n),
        out_shape=jax.ShapeDtypeStruct((n, q_dev, held), F32),
        in_specs=[spec(SMEM), spec(SMEM), spec(VMEM)] + [spec(VMEM)] * (n + 1),
        scratch_shapes=[
            VMEM((held, padded, d), BF16),
            VMEM((padded * PITCH, d), F32),
            VMEM((n * tokens, d), BF16),
            VMEM((PMOST + 32, held), I32),
            SMEM((PMOST + 32, held), I32),
            VMEM((held, PMOST * qt), F32),
            pltpu.SemaphoreType.DMA,
        ],
        compiler_params=pltpu.CompilerParams(vmem_limit_bytes=36 * MIB),
        name="score",
    )(me, lengths, lengths.reshape(1, held), *loads, passages.transpose(1, 0, 2))
    back = lax.all_to_all(dense, "shard", split_axis=0, concat_axis=0, tiled=True)
    return pl.pallas_call(
        pick_kernel, out_shape=jax.ShapeDtypeStruct((q_dev, cand), F32), name="pick"
    )(slot, back)


def solution(mesh):
    in_specs = (
        P(("groups", "shard"), None, None),
        P(("groups", "shard"), None, None),
        P(("groups", "shard")),
        P(("groups", "shard"), None),
        P("groups"),
    )
    out_specs = P(("groups", "shard"), None)
    return jax.shard_map(shards, mesh=mesh, in_specs=in_specs, out_specs=out_specs, check_vma=False)
```

```python
import functools

import jax
import jax.numpy as jnp
from jax import lax
from jax.experimental import pallas as pl
from jax.experimental.pallas import tpu as pltpu
from jax.sharding import PartitionSpec as P

PMOST = 16
LEAST = 45
PITCH = 17
LANES = 128
F32 = jnp.float32
BF16 = jnp.bfloat16
I32 = jnp.int32
NT = (((1,), (1,)), ((), ()))
NN = (((1,), (0,)), ((), ()))
VMEM = pltpu.VMEM
SMEM = pltpu.SMEM
MIB = 2**20


def iota(shape, axis):
    return lax.broadcasted_iota(I32, shape, axis)


def dot(a, b, dims, **kw):
    return lax.dot_general(a, b, dims, preferred_element_type=F32, **kw)


def lookup(table, index):
    parts = []
    for c in range(index.shape[1] // LANES):
        ids = index[:, c * LANES : (c + 1) * LANES]
        lo, hi = ids & (LANES - 1), ids >> 7
        found = jnp.zeros(ids.shape, table[0].dtype)
        for t, tile in enumerate(table):
            got = jnp.take_along_axis(tile, lo, axis=1, mode="promise_in_bounds")
            found = jnp.where(hi == t, got, found)
        parts.append(found)
    return jnp.concatenate(parts, axis=1)


def route_kernel(queries_ref, cand_ref, place_ref, slot_ref, load_ref):
    q_dev, cand = cand_ref.shape
    rows = place_ref.shape[0]
    tokens = queries_ref.shape[0]
    table = [jnp.broadcast_to(place_ref[t : t + 1, :], (q_dev, LANES)) for t in range(rows)]
    slot = lookup(table, cand_ref[...])
    slot_ref[...] = slot
    bits = jnp.zeros((rows, LANES), F32)
    for q in range(q_dev):
        line = slot[q : q + 1, :]
        hi = jnp.where(iota((rows, cand), 0) == (line >> 7), 1.0, 0.0).astype(BF16)
        lo = jnp.where(iota((LANES, cand), 0) == (line & (LANES - 1)), 1.0, 0.0).astype(BF16)
        bits = bits + jnp.where(dot(hi, lo, NT) > 0.5, float(2**q), 0.0)
    load_ref[:tokens, :] = queries_ref[...]
    load_ref[tokens:, :] = bits.astype(BF16)


def turn(len_ref, in_ref, out_ref, wide_ref, first, last):
    tokens, _, d = in_ref.shape

    def group(g, carry):
        p0 = pl.multiple_of(g * 16, 16)
        for t in range(tokens):
            wide_ref[t * PITCH : t * PITCH + 16, :] = in_ref[t, pl.ds(p0, 16), :].astype(F32)
        for p in range(16):
            live = wide_ref[p : p + 1, :]
            length = len_ref[p0 + p]
            for t in range(0, tokens, 16):
                rows = wide_ref[pl.ds(p + t * PITCH, 16, stride=PITCH), :]
                if t + 16 > LEAST:
                    rows = jnp.where(iota((16, d), 0) < length - t, rows, live)
                out_ref[p0 + p, t : t + 16] = rows.astype(BF16)
        return carry

    lax.fori_loop(first // 16, last // 16, group, 0)


def score_kernel(n, me_ref, count_ref, len_ref, *refs):
    loads, refs = refs[:n], refs[n:]
    source_ref, out_ref, in_ref, pas_ref, wide_ref = refs[:5]
    q_ref, list_vmem, list_smem, best_ref, sems = refs[5:]
    held, padded, _ = pas_ref.shape
    parts = sems.shape[0] - 1
    step = held // parts

    def fetch(i):
        at = pl.ds(i * step, step)
        return pltpu.make_async_copy(source_ref.at[:, at], in_ref.at[:, at], sems.at[i])

    for i in range(parts):
        fetch(i).start()
    rows = n * held // LANES
    tokens = loads[0].shape[0] - rows
    per = held // LANES
    q_dev = out_ref.shape[1]
    qt = tokens // q_dev
    total = n * q_dev
    low, high = (LEAST + 15) // 16, padded // 16
    me = me_ref[0]
    size = jnp.clip((len_ref[...] + 15) // 16, low, high)
    level = iota((16, held), 0)
    member = size == level
    before = jnp.where(iota((held, held), 0) < iota((held, held), 1), 1.0, 0.0).astype(BF16)
    within = dot(jnp.where(member, 1.0, 0.0).astype(BF16), before, NN)
    less = jnp.sum(jnp.where(size < level, 1.0, 0.0), axis=1, keepdims=True)
    upto = jnp.sum(jnp.where(size <= level, 1.0, 0.0), axis=1, keepdims=True)
    place = jnp.sum(jnp.where(member, less + within, 0.0), axis=0, keepdims=True)
    order = jnp.where(iota((held, held), 0) == place.astype(I32), 1.0, 0.0)
    order16 = order.astype(BF16)

    bits = jnp.concatenate([loads[k][tokens:, :] for k in range(n)], axis=0)
    halves = []
    for h in range(per):
        pick = iota((n, n * rows), 1) == iota((n, n * rows), 0) * rows + me * per + h
        halves.append(dot(jnp.where(pick, 1.0, 0.0).astype(BF16), bits, NN))
    masks = jnp.concatenate(halves, axis=1).astype(I32)
    named = [
        (jnp.broadcast_to(masks[k : k + 1], (q_dev, held)) >> iota((q_dev, held), 0)) & 1
        for k in range(n)
    ]
    named = jnp.concatenate(named, axis=0).astype(F32)
    below = jnp.where(iota((total, total), 0) > iota((total, total), 1), 1.0, 0.0).astype(BF16)
    rank = jnp.where(named > 0.5, dot(below, named.astype(BF16), NN) + 1.0, 0.0)
    ranked = dot(rank.astype(BF16), order16, NT)
    ids = iota((total, held), 0).astype(F32)
    lines = [
        jnp.sum(jnp.where(ranked == r + 1.0, ids, 0.0), axis=0, keepdims=True) for r in range(PMOST)
    ]
    list_vmem[0:PMOST, :] = jnp.concatenate(lines, axis=0).astype(I32) * qt
    own = dot(iota((16, held), 1).astype(F32).astype(BF16), order16, NT)
    list_vmem[PMOST : PMOST + 16, :] = own.astype(I32)
    list_vmem[PMOST + 16 :, :] = jnp.broadcast_to(upto, (16, held)).astype(I32)
    copy = pltpu.make_async_copy(list_vmem, list_smem, sems.at[parts])
    copy.start()
    for k in range(n):
        q_ref[k * tokens : (k + 1) * tokens, :] = loads[k][:tokens, :]
    for i in range(parts):
        fetch(i).wait()
        turn(count_ref, in_ref, pas_ref, wide_ref, i * step, (i + 1) * step)
    copy.wait()

    def walk(size, i, carry):
        for g in (0, 8):
            best = []
            for u in range(g, g + 8):
                at = i * 16 + u
                block = jnp.concatenate(
                    [q_ref[pl.ds(pl.multiple_of(list_smem[r, at], qt), qt), :] for r in range(PMOST)],
                    axis=0,
                )
                part = pas_ref[list_smem[PMOST, at], : size * 16]
                best.append(jnp.max(dot(part, block, NT), axis=0, keepdims=True))
            at = pl.multiple_of(i * 16 + g, 8)
            best_ref[pl.ds(at, 8), :] = jnp.concatenate(best, axis=0)
        return carry

    start = 0
    for s in range(low, high + 1):
        stop = list_smem[PMOST + 16 + s, 0] // 16
        lax.fori_loop(start, stop, functools.partial(walk, s), 0)
        start = stop
    wide = PMOST * qt
    mean = jnp.where(iota((PMOST, wide), 1) // qt == iota((PMOST, wide), 0), 1.0 / qt, 0.0)
    score = dot(mean, best_ref[...], NT, precision=lax.Precision.HIGHEST)
    score = dot(score, order, NN, precision=lax.Precision.HIGHEST)
    dense = jnp.zeros((total, held), F32)
    for r in range(PMOST):
        dense = jnp.where(rank == r + 1.0, score[r : r + 1, :], dense)
    for k in range(n):
        out_ref[me ^ k] = dense[k * q_dev : (k + 1) * q_dev]


def pick_kernel(slot_ref, back_ref, out_ref):
    n, _, held = back_ref.shape
    table = [
        back_ref[s][:, h * LANES : (h + 1) * LANES] for s in range(n) for h in range(held // LANES)
    ]
    out_ref[...] = lookup(table, slot_ref[...])


def spec(space):
    return pl.BlockSpec(memory_space=space)


def swap(v, k, n):
    return lax.ppermute(v, "shard", [(i, i ^ k) for i in range(n)])


def shards(queries, passages, lengths, candidates, placement):
    n = lax.axis_size("shard")
    q_dev, qt, d = queries.shape
    held, pt, _ = passages.shape
    cand = candidates.shape[1]
    me = lax.axis_index("shard").astype(I32).reshape(1)
    rows = n * held // LANES
    tokens = q_dev * qt
    padded = (pt + 15) // 16 * 16
    slot, load = pl.pallas_call(
        route_kernel,
        out_shape=(
            jax.ShapeDtypeStruct((q_dev, cand), I32),
            jax.ShapeDtypeStruct((tokens + rows, d), BF16),
        ),
        name="route",
    )(queries.reshape(tokens, d), candidates, placement.reshape(rows, LANES))
    blocks = {0: load}
    for k in range(4, n, 4):
        blocks[k] = swap(load, k, n)
    blocks[2] = swap(load, 2, n)
    blocks[1] = swap(load, 1, n)
    for k in range(4, n, 4):
        blocks[k + 2] = swap(blocks[k], 2, n)
    for k in range(2, n, 2):
        blocks[k + 1] = swap(blocks[k], 1, n)
    loads = [blocks[k] for k in range(n)]
    dense = pl.pallas_call(
        functools.partial(score_kernel, n),
        out_shape=jax.ShapeDtypeStruct((n, q_dev, held), F32),
        in_specs=[spec(SMEM), spec(SMEM), spec(VMEM)] + [spec(VMEM)] * n + [spec(pltpu.HBM)],
        scratch_shapes=[
            VMEM((pt, held, d), BF16),
            VMEM((held, padded, d), BF16),
            VMEM((padded * PITCH, d), F32),
            VMEM((n * tokens, d), BF16),
            VMEM((PMOST + 32, held), I32),
            SMEM((PMOST + 32, held), I32),
            VMEM((held, PMOST * qt), F32),
            pltpu.SemaphoreType.DMA((5,)),
        ],
        compiler_params=pltpu.CompilerParams(vmem_limit_bytes=56 * MIB),
        name="score",
    )(me, lengths, lengths.reshape(1, held), *loads, pltpu.with_memory_space_constraint(passages.transpose(1, 0, 2), pltpu.HBM))
    back = lax.all_to_all(dense, "shard", split_axis=0, concat_axis=0, tiled=True)
    return pl.pallas_call(
        pick_kernel,
        out_shape=jax.ShapeDtypeStruct((q_dev, cand), F32),
        compiler_params=pltpu.CompilerParams(vmem_limit_bytes=8 * MIB),
        name="pick",
    )(slot, back)


def solution(mesh):
    in_specs = (
        P(("groups", "shard"), None, None),
        P(("groups", "shard"), None, None),
        P(("groups", "shard")),
        P(("groups", "shard"), None),
        P("groups"),
    )
    out_specs = P(("groups", "shard"), None)
    return jax.shard_map(shards, mesh=mesh, in_specs=in_specs, out_specs=out_specs, check_vma=False)
```

```python
import functools

import jax
import jax.numpy as jnp
from jax import lax
from jax.experimental import pallas as pl
from jax.experimental.pallas import tpu as pltpu
from jax.sharding import PartitionSpec as P

PMOST = 16
LEAST = 45
PITCH = 17
DEPTH = 48
WALK = 32
LANES = 128
F32 = jnp.float32
BF16 = jnp.bfloat16
I32 = jnp.int32
NT = (((1,), (1,)), ((), ()))
NN = (((1,), (0,)), ((), ()))
VMEM = pltpu.VMEM
SMEM = pltpu.SMEM
MIB = 2**20


def iota(shape, axis):
    return lax.broadcasted_iota(I32, shape, axis)


def dot(a, b, dims, **kw):
    return lax.dot_general(a, b, dims, preferred_element_type=F32, **kw)


def lookup(table, index):
    parts = []
    for c in range(index.shape[1] // LANES):
        ids = index[:, c * LANES : (c + 1) * LANES]
        lo, hi = ids & (LANES - 1), ids >> 7
        found = jnp.zeros(ids.shape, table[0].dtype)
        for t, tile in enumerate(table):
            got = jnp.take_along_axis(tile, lo, axis=1, mode="promise_in_bounds")
            found = jnp.where(hi == t, got, found)
        parts.append(found)
    return jnp.concatenate(parts, axis=1)


def route_kernel(queries_ref, cand_ref, place_ref, slot_ref, load_ref):
    q_dev, cand = cand_ref.shape
    rows = place_ref.shape[0]
    tokens = queries_ref.shape[0]
    table = [jnp.broadcast_to(place_ref[t : t + 1, :], (q_dev, LANES)) for t in range(rows)]
    slot = lookup(table, cand_ref[...])
    slot_ref[...] = slot
    bits = jnp.zeros((rows, LANES), F32)
    for q in range(q_dev):
        line = slot[q : q + 1, :]
        hi = jnp.where(iota((rows, cand), 0) == (line >> 7), 1.0, 0.0).astype(BF16)
        lo = jnp.where(iota((LANES, cand), 0) == (line & (LANES - 1)), 1.0, 0.0).astype(BF16)
        bits = bits + jnp.where(dot(hi, lo, NT) > 0.5, float(2**q), 0.0)
    load_ref[:tokens, :] = queries_ref[...]
    load_ref[tokens:, :] = bits.astype(BF16)


def turn(len_ref, in_ref, out_ref, wide_ref, first_ref, start, stop):
    d = in_ref.shape[2]

    def group(g, carry):
        p0 = pl.multiple_of(g * 16, 16)
        for t in range(stop - start):
            wide_ref[t * PITCH : t * PITCH + 16, :] = in_ref[start + t, pl.ds(p0, 16), :].astype(F32)
        live = first_ref[pl.ds(p0, 16), :]
        for p in range(16):
            length = len_ref[p0 + p]
            for t in range(start, stop, 16):
                rows = wide_ref[pl.ds(p + (t - start) * PITCH, 16, stride=PITCH), :]
                if t + 16 > LEAST:
                    rows = jnp.where(iota((16, d), 0) < length - t, rows, live[p : p + 1])
                out_ref[p0 + p, t : t + 16] = rows.astype(BF16)
        return carry

    lax.fori_loop(0, in_ref.shape[1] // 16, group, 0)


def score_kernel(n, me_ref, count_ref, len_ref, *refs):
    loads, refs = refs[:n], refs[n:]
    source_ref, out_ref, in_ref, pas_ref, wide_ref, first_ref = refs[:6]
    q_ref, list_vmem, list_smem, best_ref, sems = refs[6:]
    held, padded, _ = pas_ref.shape
    depth = wide_ref.shape[0] // PITCH
    starts = list(range(0, in_ref.shape[0], depth))
    stops = starts[1:] + [in_ref.shape[0]]
    parts = len(starts)

    def fetch(i):
        at = pl.ds(starts[i], stops[i] - starts[i])
        return pltpu.make_async_copy(source_ref.at[at], in_ref.at[at], sems.at[i])

    for i in range(parts):
        fetch(i).start()
    rows = n * held // LANES
    tokens = loads[0].shape[0] - rows
    per = held // LANES
    q_dev = out_ref.shape[1]
    qt = tokens // q_dev
    total = n * q_dev
    low, high = (LEAST + 15) // 16, padded // 16
    levels = list(range(min(8, high), high, 2)) + [high]
    me = me_ref[0]
    size = jnp.clip((len_ref[...] + 15) // 16, low, high)
    level = iota((16, held), 0)
    member = size == level
    before = jnp.where(iota((held, held), 0) < iota((held, held), 1), 1.0, 0.0).astype(BF16)
    within = dot(jnp.where(member, 1.0, 0.0).astype(BF16), before, NN)
    less = jnp.sum(jnp.where(size < level, 1.0, 0.0), axis=1, keepdims=True)
    upto = jnp.sum(jnp.where(size <= level, 1.0, 0.0), axis=1, keepdims=True)
    place = jnp.sum(jnp.where(member, less + within, 0.0), axis=0, keepdims=True)
    order = jnp.where(iota((held, held), 0) == place.astype(I32), 1.0, 0.0)
    order16 = order.astype(BF16)

    bits = jnp.concatenate([loads[k][tokens:, :] for k in range(n)], axis=0)
    halves = []
    for h in range(per):
        pick = iota((n, n * rows), 1) == iota((n, n * rows), 0) * rows + me * per + h
        halves.append(dot(jnp.where(pick, 1.0, 0.0).astype(BF16), bits, NN))
    masks = jnp.concatenate(halves, axis=1).astype(I32)
    named = [
        (jnp.broadcast_to(masks[k : k + 1], (q_dev, held)) >> iota((q_dev, held), 0)) & 1
        for k in range(n)
    ]
    named = jnp.concatenate(named, axis=0).astype(F32)
    below = jnp.where(iota((total, total), 0) > iota((total, total), 1), 1.0, 0.0).astype(BF16)
    rank = jnp.where(named > 0.5, dot(below, named.astype(BF16), NN) + 1.0, 0.0)
    ranked = dot(rank.astype(BF16), order16, NT)
    ids = iota((total, held), 0).astype(F32)
    lines = [
        jnp.sum(jnp.where(ranked == r + 1.0, ids, 0.0), axis=0, keepdims=True) for r in range(PMOST)
    ]
    list_vmem[0:PMOST, :] = jnp.concatenate(lines, axis=0).astype(I32) * qt
    own = dot(iota((16, held), 1).astype(F32).astype(BF16), order16, NT)
    list_vmem[PMOST : PMOST + 16, :] = own.astype(I32)
    list_vmem[PMOST + 16 :, :] = jnp.broadcast_to(upto, (16, held)).astype(I32)
    copy = pltpu.make_async_copy(list_vmem, list_smem, sems.at[parts])
    copy.start()
    for k in range(n):
        q_ref[k * tokens : (k + 1) * tokens, :] = loads[k][:tokens, :]
    for i in range(parts):
        fetch(i).wait()
        if i == 0:
            first_ref[...] = in_ref[0].astype(F32)
        turn(count_ref, in_ref, pas_ref, wide_ref, first_ref, starts[i], stops[i])
    copy.wait()

    def walk(size, i, carry):
        for g in range(0, WALK, 8):
            best = []
            for u in range(g, g + 8):
                at = i * WALK + u
                block = jnp.concatenate(
                    [q_ref[pl.ds(pl.multiple_of(list_smem[r, at], qt), qt), :] for r in range(PMOST)],
                    axis=0,
                )
                part = pas_ref[list_smem[PMOST, at], : size * 16]
                best.append(jnp.max(dot(part, block, NT), axis=0, keepdims=True))
            at = pl.multiple_of(i * WALK + g, 8)
            best_ref[pl.ds(at, 8), :] = jnp.concatenate(best, axis=0)
        return carry

    start = 0
    for s in levels:
        stop = list_smem[PMOST + 16 + s, 0] // WALK
        lax.fori_loop(start, stop, functools.partial(walk, s), 0)
        start = stop
    wide = PMOST * qt
    mean = jnp.where(iota((PMOST, wide), 1) // qt == iota((PMOST, wide), 0), 1.0 / qt, 0.0)
    best = best_ref[...]
    coarse = best.astype(BF16)
    fine = (best - coarse.astype(F32)).astype(BF16)
    mean = mean.astype(BF16)
    score = dot(mean, coarse, NT) + dot(mean, fine, NT)
    score = dot(score, order, NN, precision=lax.Precision.HIGHEST)
    dense = jnp.zeros((total, held), F32)
    for r in range(PMOST):
        dense = jnp.where(rank == r + 1.0, score[r : r + 1, :], dense)
    for k in range(n):
        out_ref[me ^ k] = dense[k * q_dev : (k + 1) * q_dev]


def pick_kernel(slot_ref, back_ref, out_ref):
    n, _, held = back_ref.shape
    table = [
        back_ref[s][:, h * LANES : (h + 1) * LANES] for s in range(n) for h in range(held // LANES)
    ]
    out_ref[...] = lookup(table, slot_ref[...])


def spec(space):
    return pl.BlockSpec(memory_space=space)


def swap(v, k, n):
    return lax.ppermute(v, "shard", [(i, i ^ k) for i in range(n)])


def shards(queries, passages, lengths, candidates, placement):
    n = lax.axis_size("shard")
    q_dev, qt, d = queries.shape
    held, pt, _ = passages.shape
    cand = candidates.shape[1]
    me = lax.axis_index("shard").astype(I32).reshape(1)
    rows = n * held // LANES
    tokens = q_dev * qt
    padded = (pt + 15) // 16 * 16
    slot, load = pl.pallas_call(
        route_kernel,
        out_shape=(
            jax.ShapeDtypeStruct((q_dev, cand), I32),
            jax.ShapeDtypeStruct((tokens + rows, d), BF16),
        ),
        name="route",
    )(queries.reshape(tokens, d), candidates, placement.reshape(rows, LANES))
    blocks = {0: load}
    for k in range(n - 4, 0, -4):
        blocks[k] = swap(load, k, n)
    for k in range(n - 4, -1, -4):
        blocks[k + 2] = swap(blocks[k], 2, n)
    for k in range(n - 2, -1, -2):
        blocks[k + 1] = swap(blocks[k], 1, n)
    loads = [blocks[k] for k in range(n)]
    dense = pl.pallas_call(
        functools.partial(score_kernel, n),
        out_shape=jax.ShapeDtypeStruct((n, q_dev, held), F32),
        in_specs=[spec(SMEM), spec(SMEM), spec(VMEM)] + [spec(VMEM)] * n + [spec(pltpu.HBM)],
        scratch_shapes=[
            VMEM((pt, held, d), BF16),
            VMEM((held, padded, d), BF16),
            VMEM((DEPTH * PITCH, d), F32),
            VMEM((held, d), F32),
            VMEM((n * tokens, d), BF16),
            VMEM((PMOST + 32, held), I32),
            SMEM((PMOST + 32, held), I32),
            VMEM((held, PMOST * qt), F32),
            pltpu.SemaphoreType.DMA(((pt + DEPTH - 1) // DEPTH + 1,)),
        ],
        compiler_params=pltpu.CompilerParams(vmem_limit_bytes=56 * MIB),
        name="score",
    )(me, lengths, lengths.reshape(1, held), *loads, pltpu.with_memory_space_constraint(passages.transpose(1, 0, 2), pltpu.HBM))
    back = lax.all_to_all(dense, "shard", split_axis=0, concat_axis=0, tiled=True)
    return pl.pallas_call(
        pick_kernel,
        out_shape=jax.ShapeDtypeStruct((q_dev, cand), F32),
        compiler_params=pltpu.CompilerParams(vmem_limit_bytes=8 * MIB),
        name="pick",
    )(slot, back)


def solution(mesh):
    in_specs = (
        P(("groups", "shard"), None, None),
        P(("groups", "shard"), None, None),
        P(("groups", "shard")),
        P(("groups", "shard"), None),
        P("groups"),
    )
    out_specs = P(("groups", "shard"), None)
    return jax.shard_map(shards, mesh=mesh, in_specs=in_specs, out_specs=out_specs, check_vma=False)
```

```python
import functools

import jax
import jax.numpy as jnp
from jax import lax
from jax.experimental import pallas as pl
from jax.experimental.pallas import tpu as pltpu
from jax.sharding import PartitionSpec as P

PMOST = 16
LEAST = 45
PITCH = 17
DEPTH = 48
WALK = 32
LANES = 128
F32 = jnp.float32
BF16 = jnp.bfloat16
I32 = jnp.int32
NT = (((1,), (1,)), ((), ()))
NN = (((1,), (0,)), ((), ()))
VMEM = pltpu.VMEM
SMEM = pltpu.SMEM
MIB = 2**20


def iota(shape, axis):
    return lax.broadcasted_iota(I32, shape, axis)


def dot(a, b, dims, **kw):
    return lax.dot_general(a, b, dims, preferred_element_type=F32, **kw)


def lookup(table, index):
    parts = []
    for c in range(index.shape[1] // LANES):
        ids = index[:, c * LANES : (c + 1) * LANES]
        lo, hi = ids & (LANES - 1), ids >> 7
        found = jnp.zeros(ids.shape, table[0].dtype)
        for t, tile in enumerate(table):
            got = jnp.take_along_axis(tile, lo, axis=1, mode="promise_in_bounds")
            found = jnp.where(hi == t, got, found)
        parts.append(found)
    return jnp.concatenate(parts, axis=1)


def route_kernel(queries_ref, cand_ref, place_ref, slot_ref, load_ref):
    q_dev, cand = cand_ref.shape
    rows = place_ref.shape[0]
    tokens = queries_ref.shape[0]
    table = [jnp.broadcast_to(place_ref[t : t + 1, :], (q_dev, LANES)) for t in range(rows)]
    slot = lookup(table, cand_ref[...])
    slot_ref[...] = slot
    bits = jnp.zeros((rows, LANES), F32)
    for q in range(q_dev):
        line = slot[q : q + 1, :]
        hi = jnp.where(iota((rows, cand), 0) == (line >> 7), 1.0, 0.0).astype(BF16)
        lo = jnp.where(iota((LANES, cand), 0) == (line & (LANES - 1)), 1.0, 0.0).astype(BF16)
        bits = bits + jnp.where(dot(hi, lo, NT) > 0.5, float(2**q), 0.0)
    load_ref[:tokens, :] = queries_ref[...]
    load_ref[tokens:, :] = bits.astype(BF16)


def turn(len_ref, in_ref, out_ref, wide_ref, first_ref, start, stop):
    d = in_ref.shape[2]

    def group(g, carry):
        p0 = pl.multiple_of(g * 16, 16)
        for t in range(stop - start):
            wide_ref[t * PITCH : t * PITCH + 16, :] = in_ref[start + t, pl.ds(p0, 16), :].astype(F32)
        live = first_ref[pl.ds(p0, 16), :]
        for p in range(16):
            length = len_ref[p0 + p]
            for t in range(start, stop, 16):
                rows = wide_ref[pl.ds(p + (t - start) * PITCH, 16, stride=PITCH), :]
                if t + 16 > LEAST:
                    rows = jnp.where(iota((16, d), 0) < length - t, rows, live[p : p + 1])
                out_ref[p0 + p, t : t + 16] = rows.astype(BF16)
        return carry

    lax.fori_loop(0, in_ref.shape[1] // 16, group, 0)


def score_kernel(n, me_ref, count_hbm, len_hbm, own_ref, *refs):
    loads, refs = (None,) + refs[: n - 1], refs[n - 1 :]
    source_ref, out_ref, in_ref, pas_ref, wide_ref, first_ref = refs[:6]
    q_ref, list_vmem, list_smem, best_ref, count_ref, len_ref, bits_ref, sems = refs[6:]
    held, padded, _ = pas_ref.shape
    depth = wide_ref.shape[0] // PITCH
    starts = list(range(0, in_ref.shape[0], depth))
    stops = starts[1:] + [in_ref.shape[0]]
    parts = len(starts)

    def fetch(i):
        at = pl.ds(starts[i], stops[i] - starts[i])
        return pltpu.make_async_copy(source_ref.at[at], in_ref.at[at], sems.at[i])

    small = [
        pltpu.make_async_copy(source, target, sems.at[parts + 1 + i])
        for i, (source, target) in enumerate(
            (
                (own_ref.at[pl.ds(own_ref.shape[0] - bits_ref.shape[0], bits_ref.shape[0])], bits_ref),
                (len_hbm, len_ref),
                (count_hbm, count_ref),
                (
                    own_ref.at[pl.ds(0, own_ref.shape[0] - bits_ref.shape[0])],
                    q_ref.at[pl.ds(0, own_ref.shape[0] - bits_ref.shape[0])],
                ),
            )
        )
    ]
    for copy in small:
        copy.start()
    for i in range(parts):
        fetch(i).start()
    rows = n * held // LANES
    tokens = own_ref.shape[0] - rows
    per = held // LANES
    q_dev = out_ref.shape[1]
    qt = tokens // q_dev
    total = n * q_dev
    low, high = (LEAST + 15) // 16, padded // 16
    levels = list(range(min(8, high), high, 2)) + [high]
    me = me_ref[0]
    for k in range(1, n):
        q_ref[k * tokens : (k + 1) * tokens, :] = loads[k][:tokens, :]
    small[0].wait()
    bits = jnp.concatenate([bits_ref[...]] + [loads[k][tokens:, :] for k in range(1, n)], axis=0)
    halves = []
    for h in range(per):
        pick = iota((n, n * rows), 1) == iota((n, n * rows), 0) * rows + me * per + h
        halves.append(dot(jnp.where(pick, 1.0, 0.0).astype(BF16), bits, NN))
    masks = jnp.concatenate(halves, axis=1).astype(I32)
    named = [
        (jnp.broadcast_to(masks[k : k + 1], (q_dev, held)) >> iota((q_dev, held), 0)) & 1
        for k in range(n)
    ]
    named = jnp.concatenate(named, axis=0).astype(F32)
    below = jnp.where(iota((total, total), 0) > iota((total, total), 1), 1.0, 0.0).astype(BF16)
    rank = jnp.where(named > 0.5, dot(below, named.astype(BF16), NN) + 1.0, 0.0)
    small[1].wait()
    size = jnp.clip((len_ref[...] + 15) // 16, low, high)
    level = iota((16, held), 0)
    member = size == level
    before = jnp.where(iota((held, held), 0) < iota((held, held), 1), 1.0, 0.0).astype(BF16)
    within = dot(jnp.where(member, 1.0, 0.0).astype(BF16), before, NN)
    less = jnp.sum(jnp.where(size < level, 1.0, 0.0), axis=1, keepdims=True)
    upto = jnp.sum(jnp.where(size <= level, 1.0, 0.0), axis=1, keepdims=True)
    place = jnp.sum(jnp.where(member, less + within, 0.0), axis=0, keepdims=True)
    order = jnp.where(iota((held, held), 0) == place.astype(I32), 1.0, 0.0)
    order16 = order.astype(BF16)
    ranked = dot(rank.astype(BF16), order16, NT)
    ids = iota((total, held), 0).astype(F32)
    lines = [
        jnp.sum(jnp.where(ranked == r + 1.0, ids, 0.0), axis=0, keepdims=True) for r in range(PMOST)
    ]
    list_vmem[0:PMOST, :] = jnp.concatenate(lines, axis=0).astype(I32) * qt
    own = dot(iota((16, held), 1).astype(F32).astype(BF16), order16, NT)
    list_vmem[PMOST : PMOST + 16, :] = own.astype(I32)
    list_vmem[PMOST + 16 :, :] = jnp.broadcast_to(upto, (16, held)).astype(I32)
    copy = pltpu.make_async_copy(list_vmem, list_smem, sems.at[parts])
    copy.start()
    small[2].wait()
    for i in range(parts):
        fetch(i).wait()
        if i == 0:
            first_ref[...] = in_ref[0].astype(F32)
        turn(count_ref, in_ref, pas_ref, wide_ref, first_ref, starts[i], stops[i])
    copy.wait()
    small[3].wait()

    def walk(size, i, carry):
        for g in range(0, WALK, 8):
            best = []
            for u in range(g, g + 8):
                at = i * WALK + u
                block = jnp.concatenate(
                    [q_ref[pl.ds(pl.multiple_of(list_smem[r, at], qt), qt), :] for r in range(PMOST)],
                    axis=0,
                )
                part = pas_ref[list_smem[PMOST, at], : size * 16]
                best.append(jnp.max(dot(part, block, NT), axis=0, keepdims=True))
            at = pl.multiple_of(i * WALK + g, 8)
            best_ref[pl.ds(at, 8), :] = jnp.concatenate(best, axis=0)
        return carry

    start = 0
    for s in levels:
        stop = list_smem[PMOST + 16 + s, 0] // WALK
        lax.fori_loop(start, stop, functools.partial(walk, s), 0)
        start = stop
    wide = PMOST * qt
    mean = jnp.where(iota((PMOST, wide), 1) // qt == iota((PMOST, wide), 0), 1.0 / qt, 0.0)
    best = best_ref[...]
    coarse = best.astype(BF16)
    fine = (best - coarse.astype(F32)).astype(BF16)
    mean = mean.astype(BF16)
    score = dot(mean, coarse, NT) + dot(mean, fine, NT)
    score = dot(score, order, NN, precision=lax.Precision.HIGHEST)
    dense = jnp.zeros((total, held), F32)
    for r in range(PMOST):
        dense = jnp.where(rank == r + 1.0, score[r : r + 1, :], dense)
    for k in range(n):
        out_ref[me ^ k] = dense[k * q_dev : (k + 1) * q_dev]


def pick_kernel(slot_ref, back_ref, out_ref):
    n, _, held = back_ref.shape
    table = [
        back_ref[s][:, h * LANES : (h + 1) * LANES] for s in range(n) for h in range(held // LANES)
    ]
    out_ref[...] = lookup(table, slot_ref[...])


def spec(space):
    return pl.BlockSpec(memory_space=space)


def in_hbm(x):
    return pltpu.with_memory_space_constraint(x, pltpu.HBM)


def swap(v, k, n):
    return lax.ppermute(v, "shard", [(i, i ^ k) for i in range(n)])


def shards(queries, passages, lengths, candidates, placement):
    n = lax.axis_size("shard")
    q_dev, qt, d = queries.shape
    held, pt, _ = passages.shape
    cand = candidates.shape[1]
    me = lax.axis_index("shard").astype(I32).reshape(1)
    rows = n * held // LANES
    tokens = q_dev * qt
    padded = (pt + 15) // 16 * 16
    slot, load = pl.pallas_call(
        route_kernel,
        out_shape=(
            jax.ShapeDtypeStruct((q_dev, cand), I32),
            jax.ShapeDtypeStruct((tokens + rows, d), BF16),
        ),
        name="route",
    )(queries.reshape(tokens, d), candidates, placement.reshape(rows, LANES))
    blocks = {0: load}
    for k in range(n - 4, 0, -4):
        blocks[k] = swap(load, k, n)
    for k in range(n - 4, -1, -4):
        blocks[k + 2] = swap(blocks[k], 2, n)
    for k in range(n - 2, -1, -2):
        blocks[k + 1] = swap(blocks[k], 1, n)
    loads = [blocks[k] for k in range(n)]
    dense = pl.pallas_call(
        functools.partial(score_kernel, n),
        out_shape=jax.ShapeDtypeStruct((n, q_dev, held), F32),
        in_specs=[spec(SMEM)] + [spec(pltpu.HBM)] * 3 + [spec(VMEM)] * (n - 1) + [spec(pltpu.HBM)],
        scratch_shapes=[
            VMEM((pt, held, d), BF16),
            VMEM((held, padded, d), BF16),
            VMEM((DEPTH * PITCH, d), F32),
            VMEM((held, d), F32),
            VMEM((n * tokens, d), BF16),
            VMEM((PMOST + 32, held), I32),
            SMEM((PMOST + 32, held), I32),
            VMEM((held, PMOST * qt), F32),
            SMEM((held,), I32),
            VMEM((1, held), I32),
            VMEM((rows, d), BF16),
            pltpu.SemaphoreType.DMA(((pt + DEPTH - 1) // DEPTH + 5,)),
        ],
        compiler_params=pltpu.CompilerParams(vmem_limit_bytes=30 * MIB),
        name="score",
    )(
        me,
        in_hbm(lengths),
        in_hbm(lengths.reshape(1, held)),
        in_hbm(load),
        *loads[1:],
        in_hbm(passages.transpose(1, 0, 2)),
    )
    back = lax.all_to_all(dense, "shard", split_axis=0, concat_axis=0, tiled=True)
    return pl.pallas_call(
        pick_kernel,
        out_shape=jax.ShapeDtypeStruct((q_dev, cand), F32),
        compiler_params=pltpu.CompilerParams(vmem_limit_bytes=8 * MIB),
        name="pick",
    )(slot, back)


def solution(mesh):
    in_specs = (
        P(("groups", "shard"), None, None),
        P(("groups", "shard"), None, None),
        P(("groups", "shard")),
        P(("groups", "shard"), None),
        P("groups"),
    )
    out_specs = P(("groups", "shard"), None)
    return jax.shard_map(shards, mesh=mesh, in_specs=in_specs, out_specs=out_specs, check_vma=False)
```

```python
import functools

import jax
import jax.numpy as jnp
from jax import lax
from jax.experimental import pallas as pl
from jax.experimental.pallas import tpu as pltpu
from jax.sharding import PartitionSpec as P

PMOST = 16
LEAST = 45
PITCH = 17
DEPTH = 48
WALK = 32
LANES = 128
F32 = jnp.float32
BF16 = jnp.bfloat16
I32 = jnp.int32
NT = (((1,), (1,)), ((), ()))
NN = (((1,), (0,)), ((), ()))
VMEM = pltpu.VMEM
SMEM = pltpu.SMEM
MIB = 2**20


def iota(shape, axis):
    return lax.broadcasted_iota(I32, shape, axis)


def dot(a, b, dims, **kw):
    return lax.dot_general(a, b, dims, preferred_element_type=F32, **kw)


def lookup(table, index):
    parts = []
    for c in range(index.shape[1] // LANES):
        ids = index[:, c * LANES : (c + 1) * LANES]
        lo, hi = ids & (LANES - 1), ids >> 7
        found = jnp.zeros(ids.shape, table[0].dtype)
        for t, tile in enumerate(table):
            got = jnp.take_along_axis(tile, lo, axis=1, mode="promise_in_bounds")
            found = jnp.where(hi == t, got, found)
        parts.append(found)
    return jnp.concatenate(parts, axis=1)


def route_kernel(queries_ref, cand_ref, place_ref, slot_ref, load_ref):
    q_dev, cand = cand_ref.shape
    rows = place_ref.shape[0]
    tokens = queries_ref.shape[0]
    table = [jnp.broadcast_to(place_ref[t : t + 1, :], (q_dev, LANES)) for t in range(rows)]
    slot = lookup(table, cand_ref[...])
    slot_ref[...] = slot
    bits = jnp.zeros((rows, LANES), F32)
    for q in range(q_dev):
        line = slot[q : q + 1, :]
        hi = jnp.where(iota((rows, cand), 0) == (line >> 7), 1.0, 0.0).astype(BF16)
        lo = jnp.where(iota((LANES, cand), 0) == (line & (LANES - 1)), 1.0, 0.0).astype(BF16)
        bits = bits + jnp.where(dot(hi, lo, NT) > 0.5, float(2**q), 0.0)
    load_ref[:tokens, :] = queries_ref[...]
    load_ref[tokens:, :] = bits.astype(BF16)


def turn(len_ref, in_ref, out_ref, wide_ref, first_ref, start, stop):
    d = in_ref.shape[2]

    def group(g, carry):
        p0 = pl.multiple_of(g * 16, 16)
        for t in range(stop - start):
            wide_ref[t * PITCH : t * PITCH + 16, :] = in_ref[start + t, pl.ds(p0, 16), :].astype(F32)
        live = first_ref[pl.ds(p0, 16), :]
        for p in range(16):
            length = len_ref[p0 + p]
            for t in range(start, stop, 16):
                rows = wide_ref[pl.ds(p + (t - start) * PITCH, 16, stride=PITCH), :]
                if t + 16 > LEAST:
                    rows = jnp.where(iota((16, d), 0) < length - t, rows, live[p : p + 1])
                out_ref[p0 + p, t : t + 16] = rows.astype(BF16)
        return carry

    lax.fori_loop(0, in_ref.shape[1] // 16, group, 0)


def score_kernel(n, me_ref, count_hbm, len_hbm, own_ref, *refs):
    loads, refs = (None,) + refs[: n - 1], refs[n - 1 :]
    source_ref, out_ref, in_ref, pas_ref, wide_ref, first_ref = refs[:6]
    q_ref, list_vmem, list_smem, best_ref, count_ref, len_ref, bits_ref, sems = refs[6:]
    held, padded, _ = pas_ref.shape
    depth = wide_ref.shape[0] // PITCH
    starts = list(range(0, in_ref.shape[0], depth))
    stops = starts[1:] + [in_ref.shape[0]]
    parts = len(starts)

    def fetch(i):
        at = pl.ds(starts[i], stops[i] - starts[i])
        return pltpu.make_async_copy(source_ref.at[at], in_ref.at[at], sems.at[i])

    small = [
        pltpu.make_async_copy(source, target, sems.at[parts + 1 + i])
        for i, (source, target) in enumerate(
            (
                (own_ref.at[pl.ds(own_ref.shape[0] - bits_ref.shape[0], bits_ref.shape[0])], bits_ref),
                (len_hbm, len_ref),
                (count_hbm, count_ref),
                (
                    own_ref.at[pl.ds(0, own_ref.shape[0] - bits_ref.shape[0])],
                    q_ref.at[pl.ds(0, own_ref.shape[0] - bits_ref.shape[0])],
                ),
            )
        )
    ]
    for copy in small:
        copy.start()
    for i in range(parts):
        fetch(i).start()
    rows = n * held // LANES
    tokens = own_ref.shape[0] - rows
    per = held // LANES
    q_dev = out_ref.shape[1]
    qt = tokens // q_dev
    total = n * q_dev
    low, high = (LEAST + 15) // 16, padded // 16
    levels = list(range(min(8, high), high, 2)) + [high]
    me = me_ref[0]
    for k in range(1, n):
        q_ref[k * tokens : (k + 1) * tokens, :] = loads[k][:tokens, :]
    small[0].wait()
    bits = jnp.concatenate([bits_ref[...]] + [loads[k][tokens:, :] for k in range(1, n)], axis=0)
    halves = []
    for h in range(per):
        pick = iota((n, n * rows), 1) == iota((n, n * rows), 0) * rows + me * per + h
        halves.append(dot(jnp.where(pick, 1.0, 0.0).astype(BF16), bits, NN))
    masks = jnp.concatenate(halves, axis=1).astype(I32)
    named = [
        (jnp.broadcast_to(masks[k : k + 1], (q_dev, held)) >> iota((q_dev, held), 0)) & 1
        for k in range(n)
    ]
    named = jnp.concatenate(named, axis=0).astype(F32)
    below = jnp.where(iota((total, total), 0) > iota((total, total), 1), 1.0, 0.0).astype(BF16)
    rank = jnp.where(named > 0.5, dot(below, named.astype(BF16), NN) + 1.0, 0.0)
    small[1].wait()
    size = jnp.clip((len_ref[...] + 15) // 16, low, high)
    level = iota((16, held), 0)
    member = size == level
    before = jnp.where(iota((held, held), 0) < iota((held, held), 1), 1.0, 0.0).astype(BF16)
    within = dot(jnp.where(member, 1.0, 0.0).astype(BF16), before, NN)
    less = jnp.sum(jnp.where(size < level, 1.0, 0.0), axis=1, keepdims=True)
    upto = jnp.sum(jnp.where(size <= level, 1.0, 0.0), axis=1, keepdims=True)
    place = jnp.sum(jnp.where(member, less + within, 0.0), axis=0, keepdims=True)
    order = jnp.where(iota((held, held), 0) == place.astype(I32), 1.0, 0.0)
    order16 = order.astype(BF16)
    ranked = dot(rank.astype(BF16), order16, NT)
    ids = iota((total, held), 0).astype(F32)
    lines = [
        jnp.sum(jnp.where(ranked == r + 1.0, ids, 0.0), axis=0, keepdims=True) for r in range(PMOST)
    ]
    list_vmem[0:PMOST, :] = jnp.concatenate(lines, axis=0).astype(I32) * qt
    own = dot(iota((16, held), 1).astype(F32).astype(BF16), order16, NT)
    counts = jnp.sum(jnp.where(iota((16, held), 1) == level, upto, 0.0), axis=0, keepdims=True)
    own = jnp.where(iota((8, held), 0) == 0, own[:8], counts)
    list_vmem[PMOST:, :] = own.astype(I32)
    copy = pltpu.make_async_copy(list_vmem, list_smem, sems.at[parts])
    copy.start()
    small[2].wait()
    for i in range(parts):
        fetch(i).wait()
        if i == 0:
            first_ref[...] = in_ref[0].astype(F32)
        turn(count_ref, in_ref, pas_ref, wide_ref, first_ref, starts[i], stops[i])
    copy.wait()
    small[3].wait()

    def walk(size, i, carry):
        for g in range(0, WALK, 8):
            best = []
            for u in range(g, g + 8):
                at = i * WALK + u
                block = jnp.concatenate(
                    [q_ref[pl.ds(pl.multiple_of(list_smem[r, at], qt), qt), :] for r in range(PMOST)],
                    axis=0,
                )
                part = pas_ref[list_smem[PMOST, at], : size * 16]
                best.append(jnp.max(dot(part, block, NT), axis=0, keepdims=True))
            at = pl.multiple_of(i * WALK + g, 8)
            best_ref[pl.ds(at, 8), :] = jnp.concatenate(best, axis=0)
        return carry

    start = 0
    for s in levels:
        stop = list_smem[PMOST + 1, s] // WALK
        lax.fori_loop(start, stop, functools.partial(walk, s), 0)
        start = stop
    wide = PMOST * qt
    mean = jnp.where(iota((PMOST, wide), 1) // qt == iota((PMOST, wide), 0), 1.0 / qt, 0.0)
    best = best_ref[...]
    coarse = best.astype(BF16)
    fine = (best - coarse.astype(F32)).astype(BF16)
    mean = mean.astype(BF16)
    score = dot(mean, coarse, NT) + dot(mean, fine, NT)
    pieces, rest = [], score
    for _ in range(3):
        pieces.append(rest.astype(BF16))
        rest = rest - pieces[-1].astype(F32)
    spread = dot(jnp.concatenate(pieces, axis=0), order16, NN)
    score = spread[:PMOST] + spread[PMOST : 2 * PMOST] + spread[2 * PMOST :]
    dense = jnp.zeros((total, held), F32)
    for r in range(PMOST):
        dense = jnp.where(rank == r + 1.0, score[r : r + 1, :], dense)
    for k in range(n):
        out_ref[me ^ k] = dense[k * q_dev : (k + 1) * q_dev]


def pick_kernel(slot_ref, back_ref, out_ref):
    n, _, held = back_ref.shape
    table = [
        back_ref[s][:, h * LANES : (h + 1) * LANES] for s in range(n) for h in range(held // LANES)
    ]
    out_ref[...] = lookup(table, slot_ref[...])


def spec(space):
    return pl.BlockSpec(memory_space=space)


def in_hbm(x):
    return pltpu.with_memory_space_constraint(x, pltpu.HBM)


def swap(v, k, n):
    return lax.ppermute(v, "shard", [(i, i ^ k) for i in range(n)])


def shards(queries, passages, lengths, candidates, placement):
    n = lax.axis_size("shard")
    q_dev, qt, d = queries.shape
    held, pt, _ = passages.shape
    cand = candidates.shape[1]
    me = lax.axis_index("shard").astype(I32).reshape(1)
    rows = n * held // LANES
    tokens = q_dev * qt
    padded = (pt + 15) // 16 * 16
    slot, load = pl.pallas_call(
        route_kernel,
        out_shape=(
            jax.ShapeDtypeStruct((q_dev, cand), I32),
            jax.ShapeDtypeStruct((tokens + rows, d), BF16),
        ),
        name="route",
    )(queries.reshape(tokens, d), candidates, placement.reshape(rows, LANES))
    blocks = {0: load}
    for k in range(n - 4, 0, -4):
        blocks[k] = swap(load, k, n)
    for k in range(n - 4, -1, -4):
        blocks[k + 2] = swap(blocks[k], 2, n)
    for k in range(n - 2, -1, -2):
        blocks[k + 1] = swap(blocks[k], 1, n)
    loads = [blocks[k] for k in range(n)]
    dense = pl.pallas_call(
        functools.partial(score_kernel, n),
        out_shape=jax.ShapeDtypeStruct((n, q_dev, held), F32),
        in_specs=[spec(SMEM)] + [spec(pltpu.HBM)] * 3 + [spec(VMEM)] * (n - 1) + [spec(pltpu.HBM)],
        scratch_shapes=[
            VMEM((pt, held, d), BF16),
            VMEM((held, padded, d), BF16),
            VMEM((DEPTH * PITCH, d), F32),
            VMEM((held, d), F32),
            VMEM((n * tokens, d), BF16),
            VMEM((PMOST + 8, held), I32),
            SMEM((PMOST + 8, held), I32),
            VMEM((held, PMOST * qt), F32),
            SMEM((held,), I32),
            VMEM((1, held), I32),
            VMEM((rows, d), BF16),
            pltpu.SemaphoreType.DMA(((pt + DEPTH - 1) // DEPTH + 5,)),
        ],
        compiler_params=pltpu.CompilerParams(vmem_limit_bytes=30 * MIB),
        name="score",
    )(
        me,
        in_hbm(lengths),
        in_hbm(lengths.reshape(1, held)),
        in_hbm(load),
        *loads[1:],
        in_hbm(passages.transpose(1, 0, 2)),
    )
    back = lax.all_to_all(dense, "shard", split_axis=0, concat_axis=0, tiled=True)
    return pl.pallas_call(
        pick_kernel,
        out_shape=jax.ShapeDtypeStruct((q_dev, cand), F32),
        compiler_params=pltpu.CompilerParams(vmem_limit_bytes=8 * MIB),
        name="pick",
    )(slot, back)


def solution(mesh):
    in_specs = (
        P(("groups", "shard"), None, None),
        P(("groups", "shard"), None, None),
        P(("groups", "shard")),
        P(("groups", "shard"), None),
        P("groups"),
    )
    out_specs = P(("groups", "shard"), None)
    return jax.shard_map(shards, mesh=mesh, in_specs=in_specs, out_specs=out_specs, check_vma=False)
```

```python
import functools

import jax
import jax.numpy as jnp
from jax import lax
from jax.experimental import pallas as pl
from jax.experimental.pallas import tpu as pltpu
from jax.sharding import PartitionSpec as P

PMOST = 16
LEAST = 45
PITCH = 17
DEPTH = 32
WALK = 32
LANES = 128
F32 = jnp.float32
BF16 = jnp.bfloat16
I32 = jnp.int32
NT = (((1,), (1,)), ((), ()))
NN = (((1,), (0,)), ((), ()))
VMEM = pltpu.VMEM
SMEM = pltpu.SMEM
MIB = 2**20


def iota(shape, axis):
    return lax.broadcasted_iota(I32, shape, axis)


def dot(a, b, dims, **kw):
    return lax.dot_general(a, b, dims, preferred_element_type=F32, **kw)


def lookup(table, index):
    parts = []
    for c in range(index.shape[1] // LANES):
        ids = index[:, c * LANES : (c + 1) * LANES]
        lo, hi = ids & (LANES - 1), ids >> 7
        found = jnp.zeros(ids.shape, table[0].dtype)
        for t, tile in enumerate(table):
            got = jnp.take_along_axis(tile, lo, axis=1, mode="promise_in_bounds")
            found = jnp.where(hi == t, got, found)
        parts.append(found)
    return jnp.concatenate(parts, axis=1)


def route_kernel(queries_ref, cand_ref, place_ref, slot_ref, load_ref):
    q_dev, cand = cand_ref.shape
    rows = place_ref.shape[0]
    tokens = queries_ref.shape[0]
    table = [jnp.broadcast_to(place_ref[t : t + 1, :], (q_dev, LANES)) for t in range(rows)]
    slot = lookup(table, cand_ref[...])
    slot_ref[...] = slot
    bits = jnp.zeros((rows, LANES), F32)
    for q in range(q_dev):
        line = slot[q : q + 1, :]
        hi = jnp.where(iota((rows, cand), 0) == (line >> 7), 1.0, 0.0).astype(BF16)
        lo = jnp.where(iota((LANES, cand), 0) == (line & (LANES - 1)), 1.0, 0.0).astype(BF16)
        bits = bits + jnp.where(dot(hi, lo, NT) > 0.5, float(2**q), 0.0)
    load_ref[:tokens, :] = queries_ref[...]
    load_ref[tokens:, :] = bits.astype(BF16)


def turn(len_ref, in_ref, out_ref, wide_ref, first_ref, start, stop):
    d = in_ref.shape[2]

    def group(g, carry):
        p0 = pl.multiple_of(g * 16, 16)
        for t in range(stop - start):
            wide_ref[t * PITCH : t * PITCH + 16, :] = in_ref[start + t, pl.ds(p0, 16), :].astype(F32)
        live = first_ref[pl.ds(p0, 16), :]
        for p in range(16):
            length = len_ref[p0 + p]
            for t in range(start, stop, 16):
                rows = wide_ref[pl.ds(p + (t - start) * PITCH, 16, stride=PITCH), :]
                if t + 16 > LEAST:
                    rows = jnp.where(iota((16, d), 0) < length - t, rows, live[p : p + 1])
                out_ref[p0 + p, t : t + 16] = rows.astype(BF16)
        return carry

    lax.fori_loop(0, in_ref.shape[1] // 16, group, 0)


def score_kernel(n, me_ref, count_hbm, len_hbm, own_ref, *refs):
    loads, refs = (None,) + refs[: n - 1], refs[n - 1 :]
    source_ref, out_ref, in_ref, pas_ref, wide_ref, first_ref = refs[:6]
    q_ref, list_vmem, list_smem, best_ref, count_ref, len_ref, bits_ref, sems = refs[6:]
    held, padded, _ = pas_ref.shape
    depth = wide_ref.shape[0] // PITCH
    starts = list(range(0, in_ref.shape[0], depth))
    stops = starts[1:] + [in_ref.shape[0]]
    parts = len(starts)

    def fetch(i):
        at = pl.ds(starts[i], stops[i] - starts[i])
        return pltpu.make_async_copy(source_ref.at[at], in_ref.at[at], sems.at[i])

    small = [
        pltpu.make_async_copy(source, target, sems.at[parts + 1 + i])
        for i, (source, target) in enumerate(
            (
                (own_ref.at[pl.ds(own_ref.shape[0] - bits_ref.shape[0], bits_ref.shape[0])], bits_ref),
                (len_hbm, len_ref),
                (count_hbm, count_ref),
                (
                    own_ref.at[pl.ds(0, own_ref.shape[0] - bits_ref.shape[0])],
                    q_ref.at[pl.ds(0, own_ref.shape[0] - bits_ref.shape[0])],
                ),
            )
        )
    ]
    for copy in small:
        copy.start()
    for i in range(parts):
        fetch(i).start()
    rows = n * held // LANES
    tokens = own_ref.shape[0] - rows
    per = held // LANES
    q_dev = out_ref.shape[1]
    qt = tokens // q_dev
    total = n * q_dev
    low, high = (LEAST + 15) // 16, padded // 16
    levels = list(range(min(8, high), high, 2)) + [high]
    me = me_ref[0]
    for k in range(1, n):
        q_ref[k * tokens : (k + 1) * tokens, :] = loads[k][:tokens, :]
    small[0].wait()
    bits = jnp.concatenate([bits_ref[...]] + [loads[k][tokens:, :] for k in range(1, n)], axis=0)
    halves = []
    for h in range(per):
        pick = iota((n, n * rows), 1) == iota((n, n * rows), 0) * rows + me * per + h
        halves.append(dot(jnp.where(pick, 1.0, 0.0).astype(BF16), bits, NN))
    masks = jnp.concatenate(halves, axis=1).astype(I32)
    named = [
        (jnp.broadcast_to(masks[k : k + 1], (q_dev, held)) >> iota((q_dev, held), 0)) & 1
        for k in range(n)
    ]
    named = jnp.concatenate(named, axis=0).astype(F32)
    below = jnp.where(iota((total, total), 0) > iota((total, total), 1), 1.0, 0.0).astype(BF16)
    rank = jnp.where(named > 0.5, dot(below, named.astype(BF16), NN) + 1.0, 0.0)
    small[1].wait()
    size = jnp.clip((len_ref[...] + 15) // 16, low, high)
    level = iota((16, held), 0)
    member = size == level
    before = jnp.where(iota((held, held), 0) < iota((held, held), 1), 1.0, 0.0).astype(BF16)
    within = dot(jnp.where(member, 1.0, 0.0).astype(BF16), before, NN)
    less = jnp.sum(jnp.where(size < level, 1.0, 0.0), axis=1, keepdims=True)
    upto = jnp.sum(jnp.where(size <= level, 1.0, 0.0), axis=1, keepdims=True)
    place = jnp.sum(jnp.where(member, less + within, 0.0), axis=0, keepdims=True)
    order = jnp.where(iota((held, held), 0) == place.astype(I32), 1.0, 0.0)
    order16 = order.astype(BF16)
    ranked = dot(rank.astype(BF16), order16, NT)
    ids = iota((total, held), 0).astype(F32)
    lines = [
        jnp.sum(jnp.where(ranked == r + 1.0, ids, 0.0), axis=0, keepdims=True) for r in range(PMOST)
    ]
    list_vmem[0:PMOST, :] = jnp.concatenate(lines, axis=0).astype(I32) * qt
    own = dot(iota((16, held), 1).astype(F32).astype(BF16), order16, NT)
    counts = jnp.sum(jnp.where(iota((16, held), 1) == level, upto, 0.0), axis=0, keepdims=True)
    own = jnp.where(iota((8, held), 0) == 0, own[:8], counts)
    list_vmem[PMOST:, :] = own.astype(I32)
    copy = pltpu.make_async_copy(list_vmem, list_smem, sems.at[parts])
    copy.start()
    small[2].wait()
    for i in range(parts):
        fetch(i).wait()
        if i == 0:
            first_ref[...] = in_ref[0].astype(F32)
        turn(count_ref, in_ref, pas_ref, wide_ref, first_ref, starts[i], stops[i])
    copy.wait()
    small[3].wait()

    def walk(size, i, carry):
        for g in range(0, WALK, 8):
            best = []
            for u in range(g, g + 8):
                at = i * WALK + u
                block = jnp.concatenate(
                    [q_ref[pl.ds(pl.multiple_of(list_smem[r, at], qt), qt), :] for r in range(PMOST)],
                    axis=0,
                )
                part = pas_ref[list_smem[PMOST, at], : size * 16]
                best.append(jnp.max(dot(part, block, NT), axis=0, keepdims=True))
            at = pl.multiple_of(i * WALK + g, 8)
            best_ref[pl.ds(at, 8), :] = jnp.concatenate(best, axis=0)
        return carry

    start = 0
    for s in levels:
        stop = list_smem[PMOST + 1, s] // WALK
        lax.fori_loop(start, stop, functools.partial(walk, s), 0)
        start = stop
    wide = PMOST * qt
    mean = jnp.where(iota((PMOST, wide), 1) // qt == iota((PMOST, wide), 0), 1.0 / qt, 0.0)
    best = best_ref[...]
    coarse = best.astype(BF16)
    fine = (best - coarse.astype(F32)).astype(BF16)
    mean = mean.astype(BF16)
    score = dot(mean, coarse, NT) + dot(mean, fine, NT)
    pieces, rest = [], score
    for _ in range(3):
        pieces.append(rest.astype(BF16))
        rest = rest - pieces[-1].astype(F32)
    spread = dot(jnp.concatenate(pieces, axis=0), order16, NN)
    score = spread[:PMOST] + spread[PMOST : 2 * PMOST] + spread[2 * PMOST :]
    dense = jnp.zeros((total, held), F32)
    for r in range(PMOST):
        dense = jnp.where(rank == r + 1.0, score[r : r + 1, :], dense)
    for k in range(n):
        out_ref[me ^ k] = dense[k * q_dev : (k + 1) * q_dev]


def pick_kernel(slot_ref, back_ref, out_ref):
    n, _, held = back_ref.shape
    table = [
        back_ref[s][:, h * LANES : (h + 1) * LANES] for s in range(n) for h in range(held // LANES)
    ]
    out_ref[...] = lookup(table, slot_ref[...])


def spec(space):
    return pl.BlockSpec(memory_space=space)


def in_hbm(x):
    return pltpu.with_memory_space_constraint(x, pltpu.HBM)


def swap(v, k, n):
    return lax.ppermute(v, "shard", [(i, i ^ k) for i in range(n)])


def shards(queries, passages, lengths, candidates, placement):
    n = lax.axis_size("shard")
    q_dev, qt, d = queries.shape
    held, pt, _ = passages.shape
    cand = candidates.shape[1]
    me = lax.axis_index("shard").astype(I32).reshape(1)
    rows = n * held // LANES
    tokens = q_dev * qt
    padded = (pt + 15) // 16 * 16
    slot, load = pl.pallas_call(
        route_kernel,
        out_shape=(
            jax.ShapeDtypeStruct((q_dev, cand), I32),
            jax.ShapeDtypeStruct((tokens + rows, d), BF16),
        ),
        name="route",
    )(queries.reshape(tokens, d), candidates, placement.reshape(rows, LANES))
    blocks = {0: load}
    for k in range(n - 4, 0, -4):
        blocks[k] = swap(load, k, n)
    for k in range(n - 4, -1, -4):
        blocks[k + 2] = swap(blocks[k], 2, n)
    for k in range(n - 2, -1, -2):
        blocks[k + 1] = swap(blocks[k], 1, n)
    loads = [blocks[k] for k in range(n)]
    dense = pl.pallas_call(
        functools.partial(score_kernel, n),
        out_shape=jax.ShapeDtypeStruct((n, q_dev, held), F32),
        in_specs=[spec(SMEM)] + [spec(pltpu.HBM)] * 3 + [spec(VMEM)] * (n - 1) + [spec(pltpu.HBM)],
        scratch_shapes=[
            VMEM((pt, held, d), BF16),
            VMEM((held, padded, d), BF16),
            VMEM((DEPTH * PITCH, d), F32),
            VMEM((held, d), F32),
            VMEM((n * tokens, d), BF16),
            VMEM((PMOST + 8, held), I32),
            SMEM((PMOST + 8, held), I32),
            VMEM((held, PMOST * qt), F32),
            SMEM((held,), I32),
            VMEM((1, held), I32),
            VMEM((rows, d), BF16),
            pltpu.SemaphoreType.DMA(((pt + DEPTH - 1) // DEPTH + 5,)),
        ],
        compiler_params=pltpu.CompilerParams(vmem_limit_bytes=30 * MIB),
        name="score",
    )(
        me,
        in_hbm(lengths),
        in_hbm(lengths.reshape(1, held)),
        in_hbm(load),
        *loads[1:],
        in_hbm(passages.transpose(1, 0, 2)),
    )
    back = lax.all_to_all(dense, "shard", split_axis=0, concat_axis=0, tiled=True)
    return pl.pallas_call(
        pick_kernel,
        out_shape=jax.ShapeDtypeStruct((q_dev, cand), F32),
        compiler_params=pltpu.CompilerParams(vmem_limit_bytes=8 * MIB),
        name="pick",
    )(slot, back)


def solution(mesh):
    in_specs = (
        P(("groups", "shard"), None, None),
        P(("groups", "shard"), None, None),
        P(("groups", "shard")),
        P(("groups", "shard"), None),
        P("groups"),
    )
    out_specs = P(("groups", "shard"), None)
    return jax.shard_map(shards, mesh=mesh, in_specs=in_specs, out_specs=out_specs, check_vma=False)
```
